256 devices in a mesh: row: 8 (over x, core), col: 32 (over y, z).
Axes of the slice: x: 4, y: 4, z: 8, core: 2. Of those that a mesh axis runs over, the one named last changes fastest.
Arguments:
- tokens: bfloat16 [1024, 12288], P('col', 'row'), may hold values from -6 to 6
- weight: bfloat16 [12288, 49152], P('row', 'col'), may hold values from -0.0546875 to 0.0546875
- bias: float32 [49152], P('col'), may hold values from -3 to 3
- grad_hidden: bfloat16 [1024, 49152], P('row', 'col'), may hold values from -1.1953125 to 1.1953125
Outputs:
- hidden: bfloat16 [1024, 49152], P('row', 'col')
- grad_tokens: bfloat16 [1024, 12288], P('col', 'row')
- grad_weight: bfloat16 [12288, 49152], P('row', 'col')
- grad_bias: float32 [49152], P('col')
The draws below stay inside these ranges and needn't reach their ends.
All inputs are finite; a program needn't handle non-finite values.
Results may differ from the reference program's by a relative error of at most 0.005.
Values may be sent and summed in bfloat16 or wider, within the bound.
A program may use at most 128 MiB of HBM per device.

```python
import math
import jax
import jax.numpy as jnp
from jax import lax

D = 12288
FF = 49152
TOKENS = 1024


def spiked(values, own_key, source, target, parts, factor):
    owner, partner = [(jnp.arange(values.shape[dim]) // (values.shape[dim] // parts)).reshape([-1 if axis == dim else 1 for axis in range(values.ndim)]) for dim in (source, target)]
    chosen = jax.random.permutation(own_key, parts)[partner]
    strong = (owner == chosen) | (owner == (partner + parts // 2) % parts)
    return jnp.where(strong, factor * values, values)


def block_scale(stream_key, dims, pieces, smallest, top_value):
    factor_of, own = 1.0, jax.random.fold_in(stream_key, 6)
    for axis_at, blocks in pieces:
        draws = jnp.exp(jax.random.uniform(jax.random.fold_in(own, axis_at), (blocks,), jnp.float32, smallest / len(pieces), top_value / len(pieces)))
        factor_of = factor_of * jnp.repeat(draws, dims[axis_at] // blocks).reshape([-1 if axis == axis_at else 1 for axis in range(len(dims))])
    return factor_of


def noise(rng, extent, spread, reach, cuts=(), dtype=jnp.bfloat16):
    drawn = jax.random.normal(rng, extent, jnp.float32) * spread
    if len(cuts) > 0:
        drawn = block_scale(rng, extent, cuts, -0.22, 0.18) * drawn
    return jnp.clip(drawn, min=-reach, max=reach).astype(dtype)


def heavy_noise(rng, shape, deviation, most, cuts, heavy, held_as=jnp.bfloat16):
    result = deviation * jax.random.normal(rng, shape, jnp.float32)
    if cuts:
        result = result * block_scale(rng, shape, cuts, -0.22, 0.18)
    return jnp.clip(spiked(result, jax.random.fold_in(rng, 3), *heavy), -most, most).astype(held_as)


def setup_inputs(seed: int = 0) -> dict:
    splits = jax.random.split(jax.random.key(seed), 5)
    tokens = noise(splits[0], (TOKENS, D), 1.0, 6.0, ((0, 32), (1, 8)))
    weight = noise(splits[1], (D, FF), D ** -0.5, 0.0546875, ((0, 8), (1, 32)))
    bias = noise(splits[2], (FF,), 0.5, 3.0, ((0, 32),), jnp.float32)
    grad_hidden = heavy_noise(splits[3], (TOKENS, FF), 0.2, 1.1953125, ((0, 8), (1, 32)), (1, 0, 32, 2.75))
    return {"tokens": tokens, "weight": weight, "bias": bias, "grad_hidden": grad_hidden}


coeff = math.sqrt(2.0 / math.pi)

def gelu_value(z):
    inner = coeff * (z + 0.044715 * z * z * z)
    return 0.5 * z * (1.0 + jnp.tanh(inner))

def gelu_slope(z):
    inner = coeff * (z + 0.044715 * z * z * z)
    tval = jnp.tanh(inner)
    return 0.5 * (1.0 + tval) + 0.5 * z * (1.0 - tval * tval) * coeff * (1.0 + 3.0 * 0.044715 * z * z)

def reference(tokens, weight, bias, grad_hidden):
    preact = jnp.dot(tokens, weight, preferred_element_type=jnp.float32) + bias.astype(jnp.float32)[None, :]
    hidden = gelu_value(preact).astype(jnp.bfloat16)
    slope = (grad_hidden.astype(jnp.float32) * gelu_slope(preact)).astype(jnp.bfloat16)
    grad_tokens = jnp.dot(slope, weight.T, preferred_element_type=jnp.float32).astype(jnp.bfloat16)
    grad_weight = jnp.dot(tokens.T, slope, preferred_element_type=jnp.float32).astype(jnp.bfloat16)
    grad_bias = lax.optimization_barrier(jnp.sum(slope.astype(jnp.float32), axis=0))
    return (hidden, grad_tokens, grad_weight, grad_bias)
```

```python
import functools
import math

import jax
import jax.numpy as jnp
from jax import lax
from jax.experimental import pallas as pl
from jax.experimental.pallas import tpu as pltpu
from jax.sharding import PartitionSpec as P

MESH = pl.DeviceIdType.MESH
BF = jnp.bfloat16
F32 = jnp.float32
coeff = math.sqrt(2.0 / math.pi)

OFFS = (0, 1, -1, 2, -2, 3, -3, 4)
SLOT = {d: j for j, d in enumerate(OFFS)}
NG = 8
BLK = 32
GRP = 128
W2 = 768

TICK = 3.93
START = {"A": 10.0, "B": 12.3, "C": 18.0, "D": 24.0, "E": 25.5, "F": 35.0}


def order():
    tasks = []
    for name, start in START.items():
        for j in range(NG):
            tasks.append((start + TICK * j, name, j))
    for s, t in ((1, 14.9), (2, 22.8), (3, 30.7)):
        tasks.append((t, "R", s))
    last = START["E"] + TICK * (NG - 1)
    for n in range(6):
        tasks.append((last + 1.0 + n, "H", n))
    tasks.sort()
    return [(name, j) for _, name, j in tasks]


def body(tokens, weight, bias, gh, o_hid, o_gt, o_gw, o_gb,
         wv, wt, tok, slope, ghv, hidv, own_p, ins, inr, zown, xs, xr, acc, yown, ys, yr, zs, zr, gw, gto,
         y_ss, y_rs, r_ss, r_rs, i_ss, i_rs, x_ss, x_rs, s_ss, s_rs, f_ss, f_rs, b_ss, b_rs, z_ss, z_rs, m_ss, m_rs, l_s):
    row = lax.axis_index("row")
    col = lax.axis_index("col")
    x, k = row // 2, lax.rem(row, 2)
    y, z = col // 8, lax.rem(col, 8)
    other = 1 - k

    def dev(dx=0, dy=0, dz=0, kk=None):
        kk = k if kk is None else kk
        return (lax.rem(x + dx + 4, 4) * 2 + kk, lax.rem(y + dy + 4, 4) * 8 + lax.rem(z + dz + 8, 8))

    mate = dev(kk=other)

    def rcopy(src, dst, ss, rs, to):
        return pltpu.make_async_remote_copy(
            src_ref=src, dst_ref=dst, send_sem=ss, recv_sem=rs, device_id=to, device_id_type=MESH)

    def rows(j, b):
        return pl.ds(pl.multiple_of(j * GRP + b * BLK, BLK), BLK)

    def blk(b):
        return pl.ds(pl.multiple_of(b * BLK, BLK), BLK)

    def ymod(d):
        return lax.rem(y + d + 4, 4)

    def xmod(d):
        return lax.rem(x + d + 4, 4)

    def khalf(h):
        return pl.ds(pl.multiple_of(h * W2, W2), W2)

    sends = []

    def go(cp):
        cp.start()
        sends.append(cp)

    loads = [pltpu.make_async_copy(tokens, tok.at[rows(0, y)], l_s.at[0]),
             pltpu.make_async_copy(weight.at[:, pl.ds(0, W2)], wv.at[0], l_s.at[1]),
             pltpu.make_async_copy(weight.at[:, pl.ds(W2, W2)], wv.at[1], l_s.at[2]),
             pltpu.make_async_copy(gh.at[:, khalf(k)], ghv.at[k], l_s.at[3])]
    for cp in loads:
        cp.start()

    bar = pltpu.get_barrier_semaphore()
    peers = [mate] + [dev(dx=d) for d in (1, 2, 3)] + [dev(dy=d) for d in (1, 2, 3)] + [dev(dz=d) for d in OFFS[1:]]
    for p in peers:
        pl.semaphore_signal(bar, inc=1, device_id=p, device_id_type=MESH)
    pl.semaphore_wait(bar, len(peers))
    loads[0].wait()

    def y_copy(d):
        return rcopy(tok.at[rows(0, y)], tok.at[rows(0, y)], y_ss.at[d - 1], y_rs.at[d - 1], dev(dy=d))

    def y_arrived(d):
        b = ymod(-d)
        rcopy(tok.at[rows(0, b)], tok.at[rows(0, b)], y_ss.at[d - 1], y_rs.at[d - 1], dev(dy=d)).wait_recv()

    def ring_copy(j_from, j_to, i, to):
        b = ymod(-i)
        return rcopy(tok.at[rows(j_from, b)], tok.at[rows(j_to, b)], r_ss.at[j_to, i], r_rs.at[j_to, i], to)

    def ring_send(s, i):
        if s < 3 or i in (0, 1):
            go(ring_copy(SLOT[s], SLOT[s + 1], i, dev(dz=-1)))
        if s < 3 or i in (2, 3):
            go(ring_copy(SLOT[-s], SLOT[-s - 1] if s < 3 else SLOT[4], i, dev(dz=1)))

    def ring_arrived(j, i):
        b = ymod(-i)
        rcopy(tok.at[rows(j, b)], tok.at[rows(j, b)], r_ss.at[j, i], r_rs.at[j, i], mate).wait_recv()

    for d in (1, 3, 2):
        go(y_copy(d))
    ring_send(0, 0)
    ghx = rcopy(gh.at[:, khalf(other)], ghv.at[k], m_ss.at[0], m_rs.at[0], mate)
    go(ghx)

    loads[1].wait()
    loads[2].wait()
    for h in range(2):
        for n in range(0, 1536, 256):
            wt[h, :, n:n + 256] = wv[h, n:n + 256, :].T

    for d in (1, 3, 2):
        y_arrived(d)
        ring_send(0, d)
    loads[3].wait()
    rcopy(gh.at[:, khalf(other)], ghv.at[other], m_ss.at[0], m_rs.at[0], mate).wait_recv()
    o_gb[...] = jnp.zeros_like(o_gb)

    arrived = {0}

    def arrive(j):
        if j in arrived:
            return
        arrived.add(j)
        for i in (0, 1, 3, 2):
            ring_arrived(j, i)

    def do_r(s):
        for i in (0, 1, 3, 2):
            for j in (SLOT[s], SLOT[-s]):
                if j not in arrived:
                    ring_arrived(j, i)
            ring_send(s, i)
        arrived.update((SLOT[s], SLOT[-s]))

    def inner_copy(j):
        return rcopy(ins.at[j], inr.at[j], i_ss.at[j], i_rs.at[j], mate)

    def do_a(j):
        arrive(j)
        t = tok[j * GRP:(j + 1) * GRP, :]
        ins[j] = jnp.dot(t, wv[other], preferred_element_type=F32)
        go(inner_copy(j))
        own_p[j] = jnp.dot(t, wv[k], preferred_element_type=F32)

    def x_copy(j, d):
        return rcopy(xs.at[j, d - 1], xr.at[j, d - 1], x_ss.at[j, d - 1], x_rs.at[j, d - 1], dev(dx=d))

    def do_b(j):
        inner_copy(j).wait_recv()
        for d in (2, 1, 3):
            b = blk(xmod(d))
            xs[j, d - 1] = (own_p[j, b, :] + inr[j, b, :]).astype(BF)
            go(x_copy(j, d))
        b = blk(x)
        zown[j] = own_p[j, b, :] + inr[j, b, :]

    def s_copy(j, i, to, ss, rs, h):
        r = rows(j, xmod(-i))
        return rcopy(slope.at[h, r], slope.at[h, r], ss, rs, to)

    def do_c(j):
        pre = zown[j] + bias[pl.ds(k, 1), :]
        for d in (1, 3, 2):
            x_copy(j, d).wait_recv()
            pre = pre + xr[j, d - 1].astype(F32)
        zb = lax.rem(z + OFFS[j] + 8, 8)
        kr, at = zb // 4, blk(lax.rem(zb, 4))
        sq = pre * pre
        t = jnp.tanh(coeff * (pre + 0.044715 * pre * sq))
        hidv[kr, at, :] = (0.5 * pre * (1.0 + t)).astype(BF)
        dz = 0.5 * (1.0 + t) + 0.5 * pre * (1.0 - t * t) * coeff * (1.0 + 3.0 * 0.044715 * sq)
        slope[k, rows(j, x), :] = (ghv[kr, at, :].astype(F32) * dz).astype(BF)
        for d in (2, 1, 3):
            go(s_copy(j, 0, dev(dx=d), s_ss.at[j, d - 1], s_rs.at[j, d - 1], k))
        go(s_copy(j, 0, mate, f_ss.at[j, 0], f_rs.at[j, 0], k))

    def do_d(j):
        for d in (1, 3, 2):
            s_copy(j, d, mate, s_ss.at[j, d - 1], s_rs.at[j, d - 1], k).wait_recv()
            go(s_copy(j, d, mate, f_ss.at[j, d], f_rs.at[j, d], k))

    def b_copy(j, d):
        return rcopy(ys.at[j, d - 1], yr.at[j, d - 1], b_ss.at[j, d - 1], b_rs.at[j, d - 1], dev(dy=d))

    def do_e(j):
        for i in (0, 1, 3, 2):
            s_copy(j, i, mate, f_ss.at[j, i], f_rs.at[j, i], other).wait_recv()
        g = slice(j * GRP, (j + 1) * GRP)
        acc[...] = (jnp.dot(slope[0, g, :], wt[0], preferred_element_type=F32)
                    + jnp.dot(slope[1, g, :], wt[1], preferred_element_type=F32))
        for d in (2, 1, 3):
            ys[j, d - 1] = acc[blk(ymod(d)), :].astype(BF)
            go(b_copy(j, d))
        yown[j] = acc[blk(y), :]
        for h in range(2):
            o_gb[h:h + 1, :] += jnp.sum(slope[h, g, :].astype(F32), axis=0, keepdims=True)

    def z_copy(j):
        return rcopy(zs.at[j - 1], zr.at[j - 1], z_ss.at[j - 1], z_rs.at[j - 1], dev(dz=OFFS[j]))

    def do_f(j):
        total = yown[j]
        for d in (1, 3, 2):
            b_copy(j, d).wait_recv()
            total = total + yr[j, d - 1].astype(F32)
        if j == 0:
            yown[0] = total
        else:
            zs[j - 1] = total.astype(BF)
            go(z_copy(j))

    outs = []

    def do_h(n):
        cs = slice(n * 256, (n + 1) * 256)
        for h in range(2):
            gw[cs, h * W2:(h + 1) * W2] = lax.dot_general(
                tok[:, cs], slope[h], (((0,), (0,)), ((), ())), preferred_element_type=F32).astype(BF)
        cp = pltpu.make_async_copy(gw.at[cs, :], o_gw.at[cs, :], l_s.at[4 + n])
        cp.start()
        outs.append(cp)

    act = {"A": do_a, "B": do_b, "C": do_c, "D": do_d, "E": do_e, "F": do_f, "R": do_r, "H": do_h}
    done_c = 0
    for name, j in order():
        act[name](j)
        if name == "C":
            done_c += 1
            if done_c == NG:
                go(rcopy(hidv.at[other], o_hid.at[:, khalf(k)], m_ss.at[1], m_rs.at[1], mate))
                cp = pltpu.make_async_copy(hidv.at[k], o_hid.at[:, khalf(k)], l_s.at[10])
                cp.start()
                outs.append(cp)

    total = yown[0]
    for j in range(1, NG):
        z_copy(j).wait_recv()
        total = total + zr[j - 1].astype(F32)
    gto[...] = total.astype(BF)
    cp = pltpu.make_async_copy(gto, o_gt, l_s.at[11])
    cp.start()
    outs.append(cp)
    rcopy(hidv.at[other], o_hid.at[:, khalf(other)], m_ss.at[1], m_rs.at[1], mate).wait_recv()
    for cp in sends:
        cp.wait_send()
    for cp in outs:
        cp.wait()


def local(tokens, weight, bias, gh):
    any_ = pl.BlockSpec(memory_space=pl.ANY)
    vmem = pl.BlockSpec(memory_space=pltpu.VMEM)
    dma = pltpu.SemaphoreType.DMA
    V = pltpu.VMEM
    hid, gt, gw, gb = pl.pallas_call(
        body,
        out_shape=(jax.ShapeDtypeStruct((128, 1536), BF), jax.ShapeDtypeStruct((32, 1536), BF),
                   jax.ShapeDtypeStruct((1536, 1536), BF), jax.ShapeDtypeStruct((2, W2), F32)),
        in_specs=[any_, any_, vmem, any_],
        out_specs=(any_, any_, any_, vmem),
        scratch_shapes=[
            V((2, 1536, W2), BF), V((2, W2, 1536), BF), V((1024, 1536), BF), V((2, 1024, W2), BF),
            V((2, 128, W2), BF), V((2, 128, W2), BF),
            V((NG, GRP, W2), F32), V((NG, GRP, W2), F32), V((NG, GRP, W2), F32), V((NG, BLK, W2), F32),
            V((NG, 3, BLK, W2), BF), V((NG, 3, BLK, W2), BF), V((GRP, 1536), F32), V((NG, BLK, 1536), F32),
            V((NG, 3, BLK, 1536), BF), V((NG, 3, BLK, 1536), BF), V((NG - 1, BLK, 1536), BF), V((NG - 1, BLK, 1536), BF),
            V((1536, 1536), BF), V((BLK, 1536), BF),
            dma((3,)), dma((3,)), dma((NG, 4)), dma((NG, 4)), dma((NG,)), dma((NG,)), dma((NG, 3)), dma((NG, 3)),
            dma((NG, 3)), dma((NG, 3)), dma((NG, 4)), dma((NG, 4)), dma((NG, 3)), dma((NG, 3)),
            dma((NG - 1,)), dma((NG - 1,)), dma((2,)), dma((2,)), dma((12,)),
        ],
        compiler_params=pltpu.CompilerParams(collective_id=0, has_side_effects=True, vmem_limit_bytes=58 * 2**20),
        cost_estimate=pl.CostEstimate(flops=6 * 1024 * 1536 * 1536, bytes_accessed=10 * 2**20, transcendentals=128 * 1536),
        name="layer",
    )(tokens, weight, bias.reshape(2, W2), gh)
    return hid, gt, gw, gb.reshape(1536)


def solution(mesh):
    in_specs = (P("col", "row"), P("row", "col"), P("col"), P("row", "col"))
    out_specs = (P("row", "col"), P("col", "row"), P("row", "col"), P("col"))
    return jax.shard_map(local, mesh=mesh, in_specs=in_specs, out_specs=out_specs, check_vma=False)
```

```python
import math

import jax
import jax.numpy as jnp
from jax import lax
from jax.experimental import pallas as pl
from jax.experimental.pallas import tpu as pltpu
from jax.sharding import PartitionSpec as P

MESH = pl.DeviceIdType.MESH
BF = jnp.bfloat16
F32 = jnp.float32
coeff = math.sqrt(2.0 / math.pi)

OFFS = (0, 1, -1, 2, -2, 3, -3, 4)
SLOT = {d: j for j, d in enumerate(OFFS)}
NG = 8
W2 = 768
POS = (0, 1, 3, 2)
MSG = ((0, 1), (1, 3), (3, 4))

ORDER = (
    ("R", 0, 1), ("K", 1), ("A", (0, 0)), ("R", 0, 2), ("R", 1, 0), ("B", (0, 0)), ("A", (0, 1)), ("R", 1, 1),
    ("K", 2), ("R", 1, 2), ("B", (0, 1)), ("A", (1, None)), ("C", (0, 0)), ("A", (2, None)), ("B", (1, None)),
    ("R", 2, 1), ("K", 3), ("B", (2, None)), ("R", 2, 2), ("A", (3, None)), ("D", (0, 0)), ("R", 2, 0), ("C", (0, 1)),
    ("R", 3, 1), ("B", (3, None)), ("K", 4), ("C", (1, None)), ("R", 3, 2), ("A", (4, None)), ("B", (4, None)),
    ("E", (0, 0)), ("C", (3, None)), ("A", (7, None)), ("A", (5, None)), ("D", (1, None)), ("B", (7, None)),
    ("A", (6, None)), ("C", (4, None)), ("E", (1, None)), ("D", (3, None)), ("B", (6, None)), ("E", (3, None)),
    ("C", (7, None)), ("D", (4, None)), ("B", (5, None)), ("R", 3, 0), ("E", (4, None)), ("C", (6, None)),
    ("F", (1, None)), ("C", (2, None)), ("D", (7, None)), ("E", (7, None)), ("C", (5, None)), ("D", (6, None)),
    ("E", (6, None)), ("D", (5, None)), ("D", (2, None)), ("D", (0, 1)), ("F", (3, None)), ("F", (4, None)),
    ("E", (5, None)), ("F", (7, None)), ("E", (2, None)), ("F", (6, None)), ("E", (0, 1)), ("F", (5, None)), ("H", 0),
    ("H", 2), ("F", (2, None)), ("H", 4), ("F", (0, 1)), ("F", (0, 0)),
)


def body(tokens, weight, bias, gh, o_hid, o_gt, o_gw, o_gb,
         wv, wt, tok, slope, ghv, hidv, own_p, ins, inr, zown, xs, xr, acc, yown, ys, yr, zs, zr, bv,
         ss, y_rs, r_rs, k_rs, ky_rs, i_rs, x_rs, s_rs, f_rs, b_rs, m_rs, l_s):
    row = lax.axis_index("row")
    col = lax.axis_index("col")
    x, k = row // 2, lax.rem(row, 2)
    y, z = col // 8, lax.rem(col, 8)
    other = 1 - k

    def dev(dx=0, dy=0, dz=0, kk=None):
        kk = k if kk is None else kk
        return (lax.rem(x + dx + 4, 4) * 2 + kk, lax.rem(y + dy + 4, 4) * 8 + lax.rem(z + dz + 8, 8))

    mate = dev(kk=other)

    def rcopy(src, dst, send, recv, to):
        return pltpu.make_async_remote_copy(
            src_ref=src, dst_ref=dst, send_sem=send, recv_sem=recv, device_id=to, device_id_type=MESH)

    def arrived(dst, recv):
        rcopy(dst, dst, ss.at[0], recv, mate).wait_recv()

    def sent(src, kind):
        rcopy(src, src, ss.at[kind], m_rs.at[0], mate).wait_send()

    def xpos(d):
        i = lax.rem(y - x - d + 8, 4)
        return i + i // 2 - 2 * (i // 3)

    def khalf(h):
        return pl.ds(pl.multiple_of(h * W2, W2), W2)

    def part(ref, it):
        j, h = it
        return ref.at[j] if h is None else ref.at[j, h]

    def block(it, p):
        j, h = it
        return (j, slice(None), p) if h is None else (j, h, p)

    loads = [pltpu.make_async_copy(tokens.at[pl.ds(0, 16)], tok.at[0, 0, 0], l_s.at[0]),
             pltpu.make_async_copy(tokens.at[pl.ds(16, 16)], tok.at[0, 1, 0], l_s.at[1]),
             pltpu.make_async_copy(weight.at[:, pl.ds(0, W2)], wv.at[0], l_s.at[2]),
             pltpu.make_async_copy(weight.at[:, pl.ds(W2, W2)], wv.at[1], l_s.at[3]),
             pltpu.make_async_copy(gh.at[:, khalf(k)], ghv.at[k], l_s.at[4])]
    for cp in loads:
        cp.start()

    bar = pltpu.get_barrier_semaphore()
    peers = [dev(dz=d) for d in (4, 3, -3, 2, -2)] + [dev(dx=d) for d in (2, 1, 3)] + [dev(dy=d) for d in (2, 1, 3)]
    peers += [dev(dz=1), dev(dz=-1), mate]
    for p in peers:
        pl.semaphore_signal(bar, inc=1, device_id=p, device_id_type=MESH)
    pl.semaphore_wait(bar, len(peers))
    loads[0].wait()
    loads[1].wait()

    def ya_send(d):
        rcopy(tok.at[0, 0, 0], tok.at[0, 0, POS[d]], ss.at[0], y_rs.at[d // 2 * (3 - d)], dev(dy=d)).start()

    def ring_send(s, m):
        if s < 3:
            ps = pl.ds(MSG[m][0], MSG[m][1] - MSG[m][0])
            for sign in (1, -1):
                j = SLOT[sign * (s + 1)]
                rcopy(tok.at[SLOT[sign * s], 0, ps], tok.at[j, 0, ps], ss.at[1], r_rs.at[j, m], dev(dz=-sign)).start()
        elif m > 0:
            ps, sign = (pl.ds(0, 2), 1) if m == 1 else (pl.ds(2, 2), -1)
            for q in (m - 1, m):
                ring_wait(SLOT[sign * 3], q)
            rcopy(tok.at[SLOT[sign * 3], 0, ps], tok.at[7, 0, ps], ss.at[1], r_rs.at[7, m], dev(dz=-sign)).start()

    def k_send(s):
        for sign in (1, -1):
            if s < 3:
                j = SLOT[sign * (s + 1)]
                rcopy(tok.at[SLOT[sign * s], 1, 0], tok.at[j, 1, 0], ss.at[2], k_rs.at[j], dev(dz=-sign)).start()
            else:
                cs = pl.ds(0 if sign > 0 else W2, W2)
                rcopy(tok.at[SLOT[sign * s], 1, 0, :, cs], tok.at[7, 1, 0, :, cs], ss.at[2], k_rs.at[7],
                      dev(dz=-sign)).start()

    def ky_send(j):
        for d in (2, 1, 3):
            rcopy(tok.at[j, 1, 0], tok.at[j, 1, POS[d]], ss.at[3], ky_rs.at[j], dev(dy=d)).start()

    for d in (2, 1, 3):
        ya_send(d)
    ring_send(0, 0)
    k_send(0)
    ky_send(0)
    rcopy(gh.at[:, khalf(other)], ghv.at[k], ss.at[10], m_rs.at[0], mate).start()

    loads[2].wait()
    loads[3].wait()

    @pl.loop(0, 6)
    def _(n):
        ns = pl.ds(pl.multiple_of(n * 256, 256), 256)
        for h in range(2):
            wt[h, :, ns] = wv[h, ns, :].T

    bv[0, :] = jnp.where(k == 0, bias[0:W2], bias[W2:2 * W2])
    o_gb[...] = jnp.zeros_like(o_gb)
    loads[4].wait()

    waited = set()

    def ring_wait(j, m):
        if (j, m) in waited:
            return
        waited.add((j, m))
        if j == 0:
            arrived(tok.at[0, 0, pl.ds(1, 2)] if m == 1 else tok.at[0, 0, 3], y_rs.at[m - 1])
        elif j == 7:
            arrived(tok.at[7, 0, pl.ds(0, 2)] if m == 1 else tok.at[7, 0, pl.ds(2, 2)], r_rs.at[7, m])
        else:
            arrived(tok.at[j, 0, pl.ds(MSG[m][0], MSG[m][1] - MSG[m][0])], r_rs.at[j, m])

    def k_wait(j):
        if (j, 3) not in waited:
            waited.add((j, 3))
            arrived(tok.at[j, 1, 0], k_rs.at[j])

    def do_r(s, m):
        for j in {SLOT[s]: 0, SLOT[-s]: 0}:
            ring_wait(j, m)
        ring_send(s, m)

    def do_k(s):
        js = (SLOT[s], SLOT[-s]) if s < 4 else (7,)
        for j in js:
            k_wait(j)
        if s < 4:
            k_send(s)
        for j in js:
            ky_send(j)

    def do_a(it):
        j, h = it
        if h != 1:
            for m in range(3):
                if not (j in (0, 7) and m == 0):
                    ring_wait(j, m)
        if h != 0:
            if j > 0:
                k_wait(j)
            arrived(tok.at[j, 1, pl.ds(1, 3)], ky_rs.at[j])
        t = part(tok, it)[...].reshape(-1, 1536)
        shape = own_p.shape[1:] if h is None else own_p.shape[2:]
        part(ins, it)[...] = jnp.dot(t, wv[other], preferred_element_type=F32).reshape(shape)
        rcopy(part(ins, it), part(inr, it), ss.at[4], i_rs.at[it_at[it]], mate).start()
        part(own_p, it)[...] = jnp.dot(t, wv[k], preferred_element_type=F32).reshape(shape)

    def do_b(it):
        j, h = it
        arrived(part(inr, it), i_rs.at[it_at[it]])
        for d in (2, 1, 3):
            b = block(it, xpos(d))
            at = (j, d - 1) if h is None else (j, d - 1, h)
            xs[at] = (own_p[b] + inr[b]).astype(BF)
            rcopy(xs.at[at], xr.at[at], ss.at[5], x_rs.at[it_at[it]], dev(dx=d)).start()
        b = block(it, xpos(0))
        part(zown, it)[...] = own_p[b] + inr[b]

    def do_c(it):
        j, h = it
        arrived(xr.at[j] if h is None else xr.at[j, :, h], x_rs.at[it_at[it]])
        pre = part(zown, it)[...].reshape(-1, W2) + bv[...]
        for d in (1, 3, 2):
            at = (j, d - 1) if h is None else (j, d - 1, h)
            pre = pre + xr[at].reshape(-1, W2).astype(F32)
        zb = lax.rem(z + OFFS[j] + 8, 8)
        n, off = (32, 0) if h is None else (16, 16 * h)
        kr, rows = zb // 4, pl.ds(pl.multiple_of(lax.rem(zb, 4) * 32 + off, 16), n)
        sq = pre * pre
        t = jnp.tanh(coeff * (pre + 0.044715 * pre * sq))
        dz = 0.5 * (1.0 + t) + 0.5 * pre * (1.0 - t * t) * coeff * (1.0 + 3.0 * 0.044715 * sq)
        s = (ghv[kr, rows, :].astype(F32) * dz).astype(BF)
        b = (k,) + block(it, xpos(0))
        slope[b] = s.reshape((2, 16, W2) if h is None else (16, W2))
        for d in (2, 1, 3):
            rcopy(slope.at[b], slope.at[b], ss.at[6], s_rs.at[it_at[it]], dev(dx=d)).start()
        hidv[kr, rows, :] = (0.5 * pre * (1.0 + t)).astype(BF)

    def do_d(it):
        arrived(slope.at[(k,) + block(it, slice(0, 3))], s_rs.at[it_at[it]])
        mine = part(slope.at[k], it)
        rcopy(mine, mine, ss.at[7], f_rs.at[it_at[it]], mate).start()

    def do_e(it):
        j, h = it
        arrived(part(slope.at[other], it), f_rs.at[it_at[it]])
        s = [part(slope.at[q], it)[...].reshape(-1, W2) for q in range(2)]
        acc[0:s[0].shape[0], :] = (jnp.dot(s[0], wt[0], preferred_element_type=F32)
                                   + jnp.dot(s[1], wt[1], preferred_element_type=F32))
        halves = (0, 1) if h is None else (h,)
        for d in (2, 1, 3):
            for i, q in enumerate(halves):
                r = i * 64 + POS[4 - d] * 16
                ys[j, d - 1, q] = acc[r:r + 16, :].astype(BF)
            at = (j, d - 1) if h is None else (j, d - 1, h)
            rcopy(ys.at[at], yr.at[at], ss.at[8], b_rs.at[it_at[it]], dev(dy=d)).start()
        for i, q in enumerate(halves):
            yown[j, q] = acc[i * 64:i * 64 + 16, :]
        for q in range(2):
            o_gb[q:q + 1, :] += jnp.sum(s[q].astype(F32), axis=0, keepdims=True)

    def do_f(it):
        j, h = it
        arrived(yr.at[j] if h is None else yr.at[j, :, h], b_rs.at[it_at[it]])
        total = part(yown, it)[...]
        for d in (1, 3, 2):
            total = total + yr[(j, d - 1) if h is None else (j, d - 1, h)].astype(F32)
        if j == 0:
            part(yown, it)[...] = total
        else:
            zs[j - 1] = total.astype(BF)
            rcopy(zs.at[j - 1], zr.at[j - 1], ss.at[9], m_rs.at[2], dev(dz=OFFS[j])).start()

    def do_h(first):
        @pl.loop(first, first + 2)
        def _(n):
            cs = pl.ds(pl.multiple_of(n * 256, 256), 256)
            t = tok[:, :, :, :, cs].reshape(1024, 256)
            for h in range(2):
                o_gw[cs, h * W2:(h + 1) * W2] = lax.dot_general(
                    t, slope[h].reshape(1024, W2), (((0,), (0,)), ((), ())), preferred_element_type=F32).astype(BF)

    it_at = {it: n for n, it in enumerate(dict.fromkeys(task[1] for task in ORDER if task[0] == "A"))}
    act = {"A": do_a, "B": do_b, "C": do_c, "D": do_d, "E": do_e, "F": do_f, "R": do_r, "K": do_k, "H": do_h}
    left = len(it_at)
    first_c = True
    for task in ORDER:
        if task[0] == "C" and first_c:
            first_c = False
            arrived(ghv.at[other], m_rs.at[0])
        act[task[0]](*task[1:])
        left -= task[0] == "C"
        if task[0] == "C" and left == 0:
            rcopy(hidv.at[other], o_hid.at[:, khalf(k)], ss.at[11], m_rs.at[1], mate).start()
            o_hid[:, khalf(k)] = hidv[k]

    arrived(o_hid.at[:, khalf(other)], m_rs.at[1])
    sent(tok.at[0, 0, pl.ds(1, 3)], 0)
    sent(tok.at[pl.ds(1, 7), 0], 1)
    sent(tok.at[pl.ds(1, 7), 1, 0], 2)
    sent(tok.at[:, 1, pl.ds(1, 3)], 3)
    sent(ins, 4)
    sent(xs, 5)
    sent(slope.at[0, :, :, pl.ds(0, 3)], 6)
    sent(slope.at[0], 7)
    sent(ys, 8)
    sent(ghv.at[0], 10)
    sent(hidv.at[0], 11)
    total = yown[0]
    arrived(zr, m_rs.at[2])
    for j in range(1, NG):
        total = total + zr[j - 1].astype(F32)
    o_gt[...] = total.reshape(32, 1536).astype(BF)
    sent(zs, 9)


def put(hid, gt, gw, gb, o_hid, o_gt, o_gw, o_gb, sems):
    copies = [pltpu.make_async_copy(src, dst, sems.at[i])
              for i, (src, dst) in enumerate(((gw, o_gw), (hid, o_hid), (gt, o_gt)))]
    for cp in copies:
        cp.start()
    for h in range(2):
        o_gb[h * W2:(h + 1) * W2] = gb[h, :]
    for cp in copies:
        cp.wait()


def local(tokens, weight, bias, gh):
    any_ = pl.BlockSpec(memory_space=pl.ANY)
    vmem = pl.BlockSpec(memory_space=pltpu.VMEM)
    dma = pltpu.SemaphoreType.DMA
    V = pltpu.VMEM
    held = pl.pallas_call(
        body,
        out_shape=(V((128, 1536), BF), V((32, 1536), BF), V((1536, 1536), BF), V((2, W2), F32)),
        in_specs=[any_, any_, vmem, any_],
        out_specs=(vmem,) * 4,
        scratch_shapes=[
            V((2, 1536, W2), BF), V((2, W2, 1536), BF), V((NG, 2, 4, 16, 1536), BF), V((2, NG, 2, 4, 16, W2), BF),
            V((2, 128, W2), BF), V((2, 128, W2), BF),
            V((NG, 2, 4, 16, W2), F32), V((NG, 2, 4, 16, W2), F32), V((NG, 2, 4, 16, W2), F32), V((NG, 2, 16, W2), F32),
            V((NG, 3, 2, 16, W2), BF), V((NG, 3, 2, 16, W2), BF), V((128, 1536), F32), V((NG, 2, 16, 1536), F32),
            V((NG, 3, 2, 16, 1536), BF), V((NG, 3, 2, 16, 1536), BF),
            V((NG - 1, 2, 16, 1536), BF), V((NG - 1, 2, 16, 1536), BF), V((1, W2), F32),
            dma((12,)), dma((2,)), dma((NG, 3)), dma((NG,)), dma((NG,)),
            dma((9,)), dma((9,)), dma((9,)), dma((9,)), dma((9,)), dma((3,)), dma((5,)),
        ],
        compiler_params=pltpu.CompilerParams(collective_id=0, has_side_effects=True, vmem_limit_bytes=58 * 2**20),
        cost_estimate=pl.CostEstimate(flops=6 * 1024 * 1536 * 1536, bytes_accessed=10 * 2**20, transcendentals=128 * 1536),
        name="layer",
    )(tokens, weight, bias, gh)
    held = [pltpu.with_memory_space_constraint(v, pltpu.VMEM) for v in held]
    return pl.pallas_call(
        put,
        out_shape=(jax.ShapeDtypeStruct((128, 1536), BF), jax.ShapeDtypeStruct((32, 1536), BF),
                   jax.ShapeDtypeStruct((1536, 1536), BF), jax.ShapeDtypeStruct((2 * W2,), F32)),
        in_specs=[vmem] * 4,
        out_specs=(any_, any_, any_, vmem),
        scratch_shapes=[dma((3,))],
        compiler_params=pltpu.CompilerParams(vmem_limit_bytes=2 * 2**20),
        name="put",
    )(*held)


def solution(mesh):
    in_specs = (P("col", "row"), P("row", "col"), P("col"), P("row", "col"))
    out_specs = (P("row", "col"), P("col", "row"), P("row", "col"), P("col"))
    return jax.shard_map(local, mesh=mesh, in_specs=in_specs, out_specs=out_specs, check_vma=False)
```

```python
import math

import jax
import jax.numpy as jnp
from jax import lax
from jax.experimental import pallas as pl
from jax.experimental.pallas import tpu as pltpu
from jax.sharding import PartitionSpec as P

MESH = pl.DeviceIdType.MESH
BF = jnp.bfloat16
F32 = jnp.float32
coeff = math.sqrt(2.0 / math.pi)

OFFS = (0, 1, -1, 2, -2, 3, -3, 4)
SLOT = {d: j for j, d in enumerate(OFFS)}
NG = 8
W2 = 768
POS = (0, 1, 3, 2)
MSG = ((0, 1), (1, 3), (3, 4))

ORDER = (
    ("R", 0, 1), ("K", 1), ("A", (0, 0)), ("R", 0, 2), ("R", 1, 0), ("B", (0, 0)), ("R", 1, 1), ("K", 2),
    ("A", (1, None)), ("R", 1, 2), ("R", 2, 0), ("C", (0, 0)), ("B", (1, None)), ("A", (2, None)), ("R", 2, 1),
    ("K", 3), ("A", (3, None)), ("R", 2, 2), ("B", (2, None)), ("A", (4, None)), ("D", (0, 0)), ("C", (1, None)),
    ("R", 3, 1), ("B", (4, None)), ("A", (5, None)), ("K", 4), ("R", 3, 2), ("A", (6, None)), ("B", (5, None)),
    ("D", (1, None)), ("B", (6, None)), ("C", (4, None)), ("A", (7, None)), ("E", (1, None)), ("C", (5, None)),
    ("R", 3, 0), ("B", (7, None)), ("E", (0, 0)), ("C", (6, None)), ("A", (0, 1)), ("D", (4, None)), ("E", (4, None)),
    ("B", (3, None)), ("B", (0, 1)), ("D", (5, None)), ("E", (5, None)), ("D", (6, None)), ("C", (7, None)),
    ("C", (3, None)), ("C", (2, None)), ("C", (0, 1)), ("E", (6, None)), ("F", (4, None)), ("F", (1, None)),
    ("D", (7, None)), ("E", (7, None)), ("F", (5, None)), ("D", (3, None)), ("E", (3, None)), ("D", (0, 1)),
    ("D", (2, None)), ("F", (6, None)), ("E", (2, None)), ("F", (0, 0)), ("E", (0, 1)), ("F", (7, None)), ("H", 0),
    ("F", (3, None)), ("H", 2), ("F", (2, None)), ("F", (0, 1)), ("H", 4),
)


def body(tokens, weight, bias, gh, o_hid, o_gt, o_gw, o_gb,
         wv, wt, tok, slope, ghv, hidv, own_p, ins, inr, zown, xs, xr, acc, yown, ys, yr, zs, zr, bv, bias1,
         ss, y_rs, r_rs, k_rs, ky_rs, i_rs, x_rs, s_rs, f_rs, b_rs, m_rs, l_s):
    row = lax.axis_index("row")
    col = lax.axis_index("col")
    x, k = row // 2, lax.rem(row, 2)
    y, z = col // 8, lax.rem(col, 8)
    other = 1 - k

    def dev(dx=0, dy=0, dz=0, kk=None):
        kk = k if kk is None else kk
        return (lax.rem(x + dx + 4, 4) * 2 + kk, lax.rem(y + dy + 4, 4) * 8 + lax.rem(z + dz + 8, 8))

    mate = dev(kk=other)

    def rcopy(src, dst, send, recv, to):
        return pltpu.make_async_remote_copy(
            src_ref=src, dst_ref=dst, send_sem=send, recv_sem=recv, device_id=to, device_id_type=MESH)

    def arrived(dst, recv):
        rcopy(dst, dst, ss.at[0], recv, mate).wait_recv()

    def sent(src, kind):
        rcopy(src, src, ss.at[kind], m_rs.at[0], mate).wait_send()

    def xpos(d):
        i = lax.rem(y - x - d + 8, 4)
        return i + i // 2 - 2 * (i // 3)

    def khalf(h):
        return pl.ds(pl.multiple_of(h * W2, W2), W2)

    def part(ref, it):
        j, h = it
        return ref.at[j] if h is None else ref.at[j, h]

    def block(it, p):
        j, h = it
        return (j, slice(None), p) if h is None else (j, h, p)

    loads = [pltpu.make_async_copy(tokens.at[pl.ds(0, 16)], tok.at[0, 0, 0], l_s.at[0]),
             pltpu.make_async_copy(tokens.at[pl.ds(16, 16)], tok.at[0, 1, 0], l_s.at[1]),
             pltpu.make_async_copy(weight.at[:, pl.ds(0, W2)], wv.at[0], l_s.at[2]),
             pltpu.make_async_copy(weight.at[:, pl.ds(W2, W2)], wv.at[1], l_s.at[3]),
             pltpu.make_async_copy(gh.at[:, khalf(k)], ghv.at[k], l_s.at[4]),
             pltpu.make_async_copy(bias, bias1, l_s.at[5])]
    for cp in loads:
        cp.start()

    bar = pltpu.get_barrier_semaphore()
    peers = [dev(dx=d) for d in (2, 1, 3)] + [dev(dy=d) for d in (2, 1, 3)]
    peers += [dev(dz=1), dev(dz=-1), mate]
    for p in peers:
        pl.semaphore_signal(bar, inc=1, device_id=p, device_id_type=MESH)
    pl.semaphore_wait(bar, len(peers))
    loads[0].wait()
    loads[1].wait()

    def ya_send(d):
        rcopy(tok.at[0, 0, 0], tok.at[0, 0, POS[d]], ss.at[0], y_rs.at[d // 2 * (3 - d)], dev(dy=d)).start()

    def ring_send(s, m):
        if s < 3:
            ps = pl.ds(MSG[m][0], MSG[m][1] - MSG[m][0])
            for sign in (1, -1):
                j = SLOT[sign * (s + 1)]
                rcopy(tok.at[SLOT[sign * s], 0, ps], tok.at[j, 0, ps], ss.at[1], r_rs.at[j, m], dev(dz=-sign)).start()
        elif m > 0:
            ps, sign = (pl.ds(0, 2), 1) if m == 1 else (pl.ds(2, 2), -1)
            for q in (m - 1, m):
                ring_wait(SLOT[sign * 3], q)
            rcopy(tok.at[SLOT[sign * 3], 0, ps], tok.at[7, 0, ps], ss.at[1], r_rs.at[7, m], dev(dz=-sign)).start()

    def k_send(s):
        for sign in (1, -1):
            if s < 3:
                j = SLOT[sign * (s + 1)]
                rcopy(tok.at[SLOT[sign * s], 1, 0], tok.at[j, 1, 0], ss.at[2], k_rs.at[j], dev(dz=-sign)).start()
            else:
                cs = pl.ds(0 if sign > 0 else W2, W2)
                rcopy(tok.at[SLOT[sign * s], 1, 0, :, cs], tok.at[7, 1, 0, :, cs], ss.at[2], k_rs.at[7],
                      dev(dz=-sign)).start()

    def ky_send(j):
        for d in (2, 1, 3):
            rcopy(tok.at[j, 1, 0], tok.at[j, 1, POS[d]], ss.at[3], ky_rs.at[j], dev(dy=d)).start()

    for d in (2, 1, 3):
        ya_send(d)
    ring_send(0, 0)
    k_send(0)
    ky_send(0)
    rcopy(gh.at[:, khalf(other)], ghv.at[k], ss.at[10], m_rs.at[0], mate).start()

    loads[2].wait()
    loads[3].wait()

    @pl.loop(0, 6)
    def _(n):
        ns = pl.ds(pl.multiple_of(n * 256, 256), 256)
        for h in range(2):
            wt[h, :, ns] = wv[h, ns, :].T

    loads[5].wait()
    bv[0, :] = jnp.where(k == 0, bias1[0:W2], bias1[W2:2 * W2])
    o_gb[...] = jnp.zeros_like(o_gb)
    loads[4].wait()

    waited = set()

    def ring_wait(j, m):
        if (j, m) in waited:
            return
        waited.add((j, m))
        if j == 0:
            arrived(tok.at[0, 0, pl.ds(1, 2)] if m == 1 else tok.at[0, 0, 3], y_rs.at[m - 1])
        elif j == 7:
            arrived(tok.at[7, 0, pl.ds(0, 2)] if m == 1 else tok.at[7, 0, pl.ds(2, 2)], r_rs.at[7, m])
        else:
            arrived(tok.at[j, 0, pl.ds(MSG[m][0], MSG[m][1] - MSG[m][0])], r_rs.at[j, m])

    def k_wait(j):
        if (j, 3) not in waited:
            waited.add((j, 3))
            arrived(tok.at[j, 1, 0], k_rs.at[j])

    def do_r(s, m):
        for j in {SLOT[s]: 0, SLOT[-s]: 0}:
            ring_wait(j, m)
        ring_send(s, m)

    def do_k(s):
        js = (SLOT[s], SLOT[-s]) if s < 4 else (7,)
        for j in js:
            k_wait(j)
        if s < 4:
            k_send(s)
        for j in js:
            ky_send(j)

    def do_a(it):
        j, h = it
        if h != 1:
            for m in range(3):
                if not (j in (0, 7) and m == 0):
                    ring_wait(j, m)
        if h != 0:
            if j > 0:
                k_wait(j)
            arrived(tok.at[j, 1, pl.ds(1, 3)], ky_rs.at[j])
        t = part(tok, it)[...].reshape(-1, 1536)
        shape = own_p.shape[1:] if h is None else own_p.shape[2:]
        part(ins, it)[...] = jnp.dot(t, wv[other], preferred_element_type=F32).reshape(shape)
        rcopy(part(ins, it), part(inr, it), ss.at[4], i_rs.at[it_at[it]], mate).start()
        part(own_p, it)[...] = jnp.dot(t, wv[k], preferred_element_type=F32).reshape(shape)

    def do_b(it):
        j, h = it
        arrived(part(inr, it), i_rs.at[it_at[it]])
        for d in (2, 1, 3):
            b = block(it, xpos(d))
            at = (j, d - 1) if h is None else (j, d - 1, h)
            xs[at] = (own_p[b] + inr[b]).astype(BF)
            rcopy(xs.at[at], xr.at[at], ss.at[5], x_rs.at[it_at[it]], dev(dx=d)).start()
        b = block(it, xpos(0))
        part(zown, it)[...] = own_p[b] + inr[b]

    def do_c(it):
        j, h = it
        arrived(xr.at[j] if h is None else xr.at[j, :, h], x_rs.at[it_at[it]])
        pre = part(zown, it)[...].reshape(-1, W2) + bv[...]
        for d in (1, 3, 2):
            at = (j, d - 1) if h is None else (j, d - 1, h)
            pre = pre + xr[at].reshape(-1, W2).astype(F32)
        zb = lax.rem(z + OFFS[j] + 8, 8)
        n, off = (32, 0) if h is None else (16, 16 * h)
        kr, rows = zb // 4, pl.ds(pl.multiple_of(lax.rem(zb, 4) * 32 + off, 16), n)
        sq = pre * pre
        t = jnp.tanh(coeff * (pre + 0.044715 * pre * sq))
        dz = 0.5 * (1.0 + t) + 0.5 * pre * (1.0 - t * t) * coeff * (1.0 + 3.0 * 0.044715 * sq)
        s = (ghv[kr, rows, :].astype(F32) * dz).astype(BF)
        b = (k,) + block(it, xpos(0))
        slope[b] = s.reshape((2, 16, W2) if h is None else (16, W2))
        for d in (2, 1, 3):
            rcopy(slope.at[b], slope.at[b], ss.at[6], s_rs.at[it_at[it]], dev(dx=d)).start()
        hidv[kr, rows, :] = (0.5 * pre * (1.0 + t)).astype(BF)

    def do_d(it):
        arrived(slope.at[(k,) + block(it, slice(0, 3))], s_rs.at[it_at[it]])
        mine = part(slope.at[k], it)
        rcopy(mine, mine, ss.at[7], f_rs.at[it_at[it]], mate).start()

    def do_e(it):
        j, h = it
        arrived(part(slope.at[other], it), f_rs.at[it_at[it]])
        s = [part(slope.at[q], it)[...].reshape(-1, W2) for q in range(2)]
        acc[0:s[0].shape[0], :] = (jnp.dot(s[0], wt[0], preferred_element_type=F32)
                                   + jnp.dot(s[1], wt[1], preferred_element_type=F32))
        halves = (0, 1) if h is None else (h,)
        for d in (2, 1, 3):
            for i, q in enumerate(halves):
                r = i * 64 + POS[4 - d] * 16
                ys[j, d - 1, q] = acc[r:r + 16, :].astype(BF)
            at = (j, d - 1) if h is None else (j, d - 1, h)
            rcopy(ys.at[at], yr.at[at], ss.at[8], b_rs.at[it_at[it]], dev(dy=d)).start()
        for i, q in enumerate(halves):
            yown[j, q] = acc[i * 64:i * 64 + 16, :]
        for q in range(2):
            o_gb[q:q + 1, :] += jnp.sum(s[q].astype(F32), axis=0, keepdims=True)

    def do_f(it):
        j, h = it
        arrived(yr.at[j] if h is None else yr.at[j, :, h], b_rs.at[it_at[it]])
        total = part(yown, it)[...]
        for d in (1, 3, 2):
            total = total + yr[(j, d - 1) if h is None else (j, d - 1, h)].astype(F32)
        if j == 0:
            part(yown, it)[...] = total
        else:
            zs[j - 1] = total.astype(BF)
            rcopy(zs.at[j - 1], zr.at[j - 1], ss.at[9], m_rs.at[2], dev(dz=OFFS[j])).start()

    def do_h(first):
        @pl.loop(first, first + 2)
        def _(n):
            cs = pl.ds(pl.multiple_of(n * 256, 256), 256)
            t = tok[:, :, :, :, cs].reshape(1024, 256)
            for h in range(2):
                o_gw[cs, h * W2:(h + 1) * W2] = lax.dot_general(
                    t, slope[h].reshape(1024, W2), (((0,), (0,)), ((), ())), preferred_element_type=F32).astype(BF)

    it_at = {it: n for n, it in enumerate(dict.fromkeys(task[1] for task in ORDER if task[0] == "A"))}
    act = {"A": do_a, "B": do_b, "C": do_c, "D": do_d, "E": do_e, "F": do_f, "R": do_r, "K": do_k, "H": do_h}
    left = len(it_at)
    first_c = True
    for task in ORDER:
        if task[0] == "C" and first_c:
            first_c = False
            arrived(ghv.at[other], m_rs.at[0])
        act[task[0]](*task[1:])
        left -= task[0] == "C"
        if task[0] == "C" and left == 0:
            rcopy(hidv.at[other], o_hid.at[:, khalf(k)], ss.at[11], m_rs.at[1], mate).start()
            o_hid[:, khalf(k)] = hidv[k]

    arrived(o_hid.at[:, khalf(other)], m_rs.at[1])
    sent(tok.at[0, 0, pl.ds(1, 3)], 0)
    sent(tok.at[pl.ds(1, 7), 0], 1)
    sent(tok.at[pl.ds(1, 7), 1, 0], 2)
    sent(tok.at[:, 1, pl.ds(1, 3)], 3)
    sent(ins, 4)
    sent(xs, 5)
    sent(slope.at[0, :, :, pl.ds(0, 3)], 6)
    sent(slope.at[0], 7)
    sent(ys, 8)
    sent(ghv.at[0], 10)
    sent(hidv.at[0], 11)
    total = yown[0]
    arrived(zr, m_rs.at[2])
    for j in range(1, NG):
        total = total + zr[j - 1].astype(F32)
    o_gt[...] = total.reshape(32, 1536).astype(BF)
    sent(zs, 9)


def put(hid, gt, gw, gb, o_hid, o_gt, o_gw, o_gb, gb1, sems):
    copies = [pltpu.make_async_copy(src, dst, sems.at[i])
              for i, (src, dst) in enumerate(((gw, o_gw), (hid, o_hid), (gt, o_gt), (gb1, o_gb)))]
    for cp in copies[:3]:
        cp.start()
    for h in range(2):
        gb1[h * W2:(h + 1) * W2] = gb[h, :]
    copies[3].start()
    for cp in copies:
        cp.wait()


def local(tokens, weight, bias, gh):
    any_ = pl.BlockSpec(memory_space=pl.ANY)
    vmem = pl.BlockSpec(memory_space=pltpu.VMEM)
    dma = pltpu.SemaphoreType.DMA
    V = pltpu.VMEM
    held = pl.pallas_call(
        body,
        out_shape=(V((128, 1536), BF), V((32, 1536), BF), V((1536, 1536), BF), V((2, W2), F32)),
        in_specs=[any_] * 4,
        out_specs=(vmem,) * 4,
        scratch_shapes=[
            V((2, 1536, W2), BF), V((2, W2, 1536), BF), V((NG, 2, 4, 16, 1536), BF), V((2, NG, 2, 4, 16, W2), BF),
            V((2, 128, W2), BF), V((2, 128, W2), BF),
            V((NG, 2, 4, 16, W2), F32), V((NG, 2, 4, 16, W2), F32), V((NG, 2, 4, 16, W2), F32), V((NG, 2, 16, W2), F32),
            V((NG, 3, 2, 16, W2), BF), V((NG, 3, 2, 16, W2), BF), V((128, 1536), F32), V((NG, 2, 16, 1536), F32),
            V((NG, 3, 2, 16, 1536), BF), V((NG, 3, 2, 16, 1536), BF),
            V((NG - 1, 2, 16, 1536), BF), V((NG - 1, 2, 16, 1536), BF), V((1, W2), F32), V((2 * W2,), F32),
            dma((12,)), dma((2,)), dma((NG, 3)), dma((NG,)), dma((NG,)),
            dma((9,)), dma((9,)), dma((9,)), dma((9,)), dma((9,)), dma((3,)), dma((6,)),
        ],
        compiler_params=pltpu.CompilerParams(collective_id=0, has_side_effects=True, vmem_limit_bytes=58 * 2**20),
        cost_estimate=pl.CostEstimate(flops=6 * 1024 * 1536 * 1536, bytes_accessed=10 * 2**20, transcendentals=128 * 1536),
        name="layer",
    )(tokens, weight, bias, gh)
    held = [pltpu.with_memory_space_constraint(v, pltpu.VMEM) for v in held]
    return pl.pallas_call(
        put,
        out_shape=(jax.ShapeDtypeStruct((128, 1536), BF), jax.ShapeDtypeStruct((32, 1536), BF),
                   jax.ShapeDtypeStruct((1536, 1536), BF), jax.ShapeDtypeStruct((2 * W2,), F32)),
        in_specs=[vmem] * 4,
        out_specs=(any_,) * 4,
        scratch_shapes=[V((2 * W2,), F32), dma((4,))],
        compiler_params=pltpu.CompilerParams(vmem_limit_bytes=2 * 2**20),
        name="put",
    )(*held)


def solution(mesh):
    in_specs = (P("col", "row"), P("row", "col"), P("col"), P("row", "col"))
    out_specs = (P("row", "col"), P("col", "row"), P("row", "col"), P("col"))
    return jax.shard_map(local, mesh=mesh, in_specs=in_specs, out_specs=out_specs, check_vma=False)
```

```python
import math

import jax
import jax.numpy as jnp
from jax import lax
from jax.experimental import pallas as pl
from jax.experimental.pallas import tpu as pltpu
from jax.sharding import PartitionSpec as P

MESH = pl.DeviceIdType.MESH
BF = jnp.bfloat16
F32 = jnp.float32
coeff = math.sqrt(2.0 / math.pi)

OFFS = (0, 1, -1, 2, -2, 3, -3, 4)
SLOT = {d: j for j, d in enumerate(OFFS)}
NG = 8
W2 = 768
POS = (0, 1, 3, 2)
MSG = ((0, 1), (1, 3), (3, 4))

ORDER = (
    ("R", 0, 1), ("K", 1), ("A", (0, 0)), ("R", 0, 2), ("R", 1, 0), ("B", (0, 0)), ("R", 1, 1), ("K", 2),
    ("A", (1, None)), ("R", 1, 2), ("R", 2, 0), ("C", (0, 0)), ("B", (1, None)), ("A", (2, None)), ("R", 2, 1),
    ("K", 3), ("A", (3, None)), ("R", 2, 2), ("B", (2, None)), ("A", (4, None)), ("D", (0, 0)), ("C", (1, None)),
    ("R", 3, 1), ("B", (4, None)), ("A", (5, None)), ("K", 4), ("R", 3, 2), ("A", (6, None)), ("B", (5, None)),
    ("D", (1, None)), ("B", (6, None)), ("C", (4, None)), ("A", (7, None)), ("E", (1, None)), ("C", (5, None)),
    ("R", 3, 0), ("B", (7, None)), ("E", (0, 0)), ("C", (6, None)), ("A", (0, 1)), ("D", (4, None)), ("E", (4, None)),
    ("B", (3, None)), ("B", (0, 1)), ("D", (5, None)), ("E", (5, None)), ("D", (6, None)), ("C", (7, None)),
    ("C", (3, None)), ("C", (2, None)), ("C", (0, 1)), ("E", (6, None)), ("F", (4, None)), ("F", (1, None)),
    ("D", (7, None)), ("E", (7, None)), ("F", (5, None)), ("D", (3, None)), ("E", (3, None)), ("D", (0, 1)),
    ("D", (2, None)), ("F", (6, None)), ("E", (2, None)), ("F", (0, 0)), ("E", (0, 1)), ("F", (7, None)), ("H", 0),
    ("F", (3, None)), ("H", 2), ("F", (2, None)), ("F", (0, 1)), ("H", 4),
)


def body(tokens, weight, bias, gh, o_hid, o_gt, o_gw, o_gb,
         wv, wt, tok, slope, ghv, hidv, own_p, ins, inr, zown, xs, xr, acc, yown, ys, yr, zs, zr, bv, bias1,
         ss, y_rs, r_rs, k_rs, ky_rs, i_rs, x_rs, s_rs, f_rs, b_rs, m_rs, l_s):
    row = lax.axis_index("row")
    col = lax.axis_index("col")
    x, k = row // 2, lax.rem(row, 2)
    y, z = col // 8, lax.rem(col, 8)
    other = 1 - k

    def dev(dx=0, dy=0, dz=0, kk=None):
        kk = k if kk is None else kk
        return (lax.rem(x + dx + 4, 4) * 2 + kk, lax.rem(y + dy + 4, 4) * 8 + lax.rem(z + dz + 8, 8))

    mate = dev(kk=other)

    def rcopy(src, dst, send, recv, to):
        return pltpu.make_async_remote_copy(
            src_ref=src, dst_ref=dst, send_sem=send, recv_sem=recv, device_id=to, device_id_type=MESH)

    def arrived(dst, recv):
        rcopy(dst, dst, ss.at[0], recv, mate).wait_recv()

    def sent(src, kind):
        rcopy(src, src, ss.at[kind], m_rs.at[0], mate).wait_send()

    def xpos(d):
        i = lax.rem(y - x - d + 8, 4)
        return i + i // 2 - 2 * (i // 3)

    def khalf(h):
        return pl.ds(pl.multiple_of(h * W2, W2), W2)

    def part(ref, it):
        j, h = it
        return ref.at[j] if h is None else ref.at[j, h]

    def block(it, p):
        j, h = it
        return (j, slice(None), p) if h is None else (j, h, p)

    loads = [pltpu.make_async_copy(tokens.at[pl.ds(0, 16)], tok.at[0, 0, 0], l_s.at[0]),
             pltpu.make_async_copy(tokens.at[pl.ds(16, 16)], tok.at[0, 1, 0], l_s.at[1]),
             pltpu.make_async_copy(weight.at[:, pl.ds(0, W2)], wv.at[0], l_s.at[2]),
             pltpu.make_async_copy(weight.at[:, pl.ds(W2, W2)], wv.at[1], l_s.at[3]),
             pltpu.make_async_copy(gh.at[:, khalf(k)], ghv.at[k], l_s.at[4]),
             pltpu.make_async_copy(bias, bias1, l_s.at[5])]
    for cp in loads:
        cp.start()

    bar = pltpu.get_barrier_semaphore()
    peers = [dev(dx=d) for d in (2, 1, 3)] + [dev(dy=d) for d in (2, 1, 3)]
    peers += [dev(dz=1), dev(dz=-1), mate]
    for p in peers:
        pl.semaphore_signal(bar, inc=1, device_id=p, device_id_type=MESH)
    pl.semaphore_wait(bar, len(peers))
    loads[0].wait()
    loads[1].wait()

    def ya_send(d):
        rcopy(tok.at[0, 0, 0], tok.at[0, 0, POS[d]], ss.at[0], y_rs.at[d // 2 * (3 - d)], dev(dy=d)).start()

    def ring_send(s, m):
        if s < 3:
            ps = pl.ds(MSG[m][0], MSG[m][1] - MSG[m][0])
            for sign in (1, -1):
                j = SLOT[sign * (s + 1)]
                rcopy(tok.at[SLOT[sign * s], 0, ps], tok.at[j, 0, ps], ss.at[1], r_rs.at[j, m], dev(dz=-sign)).start()
        elif m > 0:
            ps, sign = (pl.ds(0, 2), 1) if m == 1 else (pl.ds(2, 2), -1)
            for q in (m - 1, m):
                ring_wait(SLOT[sign * 3], q)
            rcopy(tok.at[SLOT[sign * 3], 0, ps], tok.at[7, 0, ps], ss.at[1], r_rs.at[7, m], dev(dz=-sign)).start()

    def k_send(s):
        for sign in (1, -1):
            if s < 3:
                j = SLOT[sign * (s + 1)]
                rcopy(tok.at[SLOT[sign * s], 1, 0], tok.at[j, 1, 0], ss.at[2], k_rs.at[j], dev(dz=-sign)).start()
            else:
                cs = pl.ds(0 if sign > 0 else W2, W2)
                rcopy(tok.at[SLOT[sign * s], 1, 0, :, cs], tok.at[7, 1, 0, :, cs], ss.at[2], k_rs.at[7],
                      dev(dz=-sign)).start()

    def ky_send(j):
        for d in (2, 1, 3):
            rcopy(tok.at[j, 1, 0], tok.at[j, 1, POS[d]], ss.at[3], ky_rs.at[j], dev(dy=d)).start()

    k_send(0)
    for d in (2, 1, 3):
        ya_send(d)
    ring_send(0, 0)
    ky_send(0)
    rcopy(gh.at[:, khalf(other)], ghv.at[k], ss.at[10], m_rs.at[0], mate).start()

    loads[2].wait()
    loads[3].wait()

    @pl.loop(0, 6)
    def _(n):
        ns = pl.ds(pl.multiple_of(n * 256, 256), 256)
        for h in range(2):
            wt[h, :, ns] = wv[h, ns, :].T

    loads[5].wait()
    bv[0, :] = jnp.where(k == 0, bias1[0:W2], bias1[W2:2 * W2])
    o_gb[...] = jnp.zeros_like(o_gb)
    loads[4].wait()

    waited = set()

    def ring_wait(j, m):
        if (j, m) in waited:
            return
        waited.add((j, m))
        if j == 0:
            arrived(tok.at[0, 0, pl.ds(1, 2)] if m == 1 else tok.at[0, 0, 3], y_rs.at[m - 1])
        elif j == 7:
            arrived(tok.at[7, 0, pl.ds(0, 2)] if m == 1 else tok.at[7, 0, pl.ds(2, 2)], r_rs.at[7, m])
        else:
            arrived(tok.at[j, 0, pl.ds(MSG[m][0], MSG[m][1] - MSG[m][0])], r_rs.at[j, m])

    def k_wait(j):
        if (j, 3) not in waited:
            waited.add((j, 3))
            arrived(tok.at[j, 1, 0], k_rs.at[j])

    def do_r(s, m):
        for j in {SLOT[s]: 0, SLOT[-s]: 0}:
            ring_wait(j, m)
        ring_send(s, m)

    def do_k(s):
        js = (SLOT[s], SLOT[-s]) if s < 4 else (7,)
        for j in js:
            k_wait(j)
        if s < 4:
            k_send(s)
        for j in js:
            ky_send(j)

    def do_a(it):
        j, h = it
        if h != 1:
            for m in range(3):
                if not (j in (0, 7) and m == 0):
                    ring_wait(j, m)
        if h != 0:
            if j > 0:
                k_wait(j)
            arrived(tok.at[j, 1, pl.ds(1, 3)], ky_rs.at[j])
        t = part(tok, it)[...].reshape(-1, 1536)
        shape = own_p.shape[1:] if h is None else own_p.shape[2:]
        part(ins, it)[...] = jnp.dot(t, wv[other], preferred_element_type=F32).reshape(shape)
        rcopy(part(ins, it), part(inr, it), ss.at[4], i_rs.at[it_at[it]], mate).start()
        part(own_p, it)[...] = jnp.dot(t, wv[k], preferred_element_type=F32).reshape(shape)

    def do_b(it):
        j, h = it
        arrived(part(inr, it), i_rs.at[it_at[it]])
        for d in (2, 1, 3):
            b = block(it, xpos(d))
            at = (j, d - 1) if h is None else (j, d - 1, h)
            xs[at] = (own_p[b] + inr[b]).astype(BF)
            rcopy(xs.at[at], xr.at[at], ss.at[5], x_rs.at[it_at[it]], dev(dx=d)).start()
        b = block(it, xpos(0))
        part(zown, it)[...] = own_p[b] + inr[b]

    def do_c(it):
        j, h = it
        arrived(xr.at[j] if h is None else xr.at[j, :, h], x_rs.at[it_at[it]])
        pre = part(zown, it)[...].reshape(-1, W2) + bv[...]
        for d in (1, 3, 2):
            at = (j, d - 1) if h is None else (j, d - 1, h)
            pre = pre + xr[at].reshape(-1, W2).astype(F32)
        zb = lax.rem(z + OFFS[j] + 8, 8)
        n, off = (32, 0) if h is None else (16, 16 * h)
        kr, rows = zb // 4, pl.ds(pl.multiple_of(lax.rem(zb, 4) * 32 + off, 16), n)
        sq = pre * pre
        t = jnp.tanh(coeff * (pre + 0.044715 * pre * sq))
        dz = 0.5 * (1.0 + t) + 0.5 * pre * (1.0 - t * t) * coeff * (1.0 + 3.0 * 0.044715 * sq)
        s = (ghv[kr, rows, :].astype(F32) * dz).astype(BF)
        b = (k,) + block(it, xpos(0))
        slope[b] = s.reshape((2, 16, W2) if h is None else (16, W2))
        for d in (2, 1, 3):
            rcopy(slope.at[b], slope.at[b], ss.at[6], s_rs.at[it_at[it]], dev(dx=d)).start()
        hidv[kr, rows, :] = (0.5 * pre * (1.0 + t)).astype(BF)

    def do_d(it):
        arrived(slope.at[(k,) + block(it, slice(0, 3))], s_rs.at[it_at[it]])
        mine = part(slope.at[k], it)
        rcopy(mine, mine, ss.at[7], f_rs.at[it_at[it]], mate).start()

    def do_e(it):
        j, h = it
        arrived(part(slope.at[other], it), f_rs.at[it_at[it]])
        s = [part(slope.at[q], it)[...].reshape(-1, W2) for q in range(2)]
        halves = (0, 1) if h is None else (h,)
        for c in range(2):
            cs = slice(c * W2, (c + 1) * W2)
            acc[0:s[0].shape[0], cs] = (jnp.dot(s[0], wt[0, :, cs], preferred_element_type=F32)
                                        + jnp.dot(s[1], wt[1, :, cs], preferred_element_type=F32))
            for d in (2, 1, 3):
                for i, q in enumerate(halves):
                    r = i * 64 + POS[4 - d] * 16
                    ys[j, d - 1, q, :, cs] = acc[r:r + 16, cs].astype(BF)
                at = (j, d - 1) + ((slice(None),) if h is None else (h,)) + (slice(None), pl.ds(c * W2, W2))
                rcopy(ys.at[at], yr.at[at], ss.at[8], b_rs.at[it_at[it]], dev(dy=d)).start()
        for i, q in enumerate(halves):
            yown[j, q] = acc[i * 64:i * 64 + 16, :]
        for q in range(2):
            o_gb[q:q + 1, :] += jnp.sum(s[q].astype(F32), axis=0, keepdims=True)

    def do_f(it):
        j, h = it
        arrived(yr.at[j] if h is None else yr.at[j, :, h], b_rs.at[it_at[it]])
        total = part(yown, it)[...]
        for d in (1, 3, 2):
            total = total + yr[(j, d - 1) if h is None else (j, d - 1, h)].astype(F32)
        if j == 0:
            part(yown, it)[...] = total
        else:
            zs[j - 1] = total.astype(BF)
            rcopy(zs.at[j - 1], zr.at[j - 1], ss.at[9], m_rs.at[2], dev(dz=OFFS[j])).start()

    def do_h(first):
        @pl.loop(first, first + 2)
        def _(n):
            cs = pl.ds(pl.multiple_of(n * 256, 256), 256)
            t = tok[:, :, :, :, cs].reshape(1024, 256)
            for h in range(2):
                o_gw[cs, h * W2:(h + 1) * W2] = lax.dot_general(
                    t, slope[h].reshape(1024, W2), (((0,), (0,)), ((), ())), preferred_element_type=F32).astype(BF)

    it_at = {it: n for n, it in enumerate(dict.fromkeys(task[1] for task in ORDER if task[0] == "A"))}
    act = {"A": do_a, "B": do_b, "C": do_c, "D": do_d, "E": do_e, "F": do_f, "R": do_r, "K": do_k, "H": do_h}
    left = len(it_at)
    first_c = True
    for task in ORDER:
        if task[0] == "C" and first_c:
            first_c = False
            arrived(ghv.at[other], m_rs.at[0])
        act[task[0]](*task[1:])
        left -= task[0] == "C"
        if task[0] == "C" and left == 0:
            rcopy(hidv.at[other], o_hid.at[:, khalf(k)], ss.at[11], m_rs.at[1], mate).start()
            o_hid[:, khalf(k)] = hidv[k]

    arrived(o_hid.at[:, khalf(other)], m_rs.at[1])
    sent(tok.at[0, 0, pl.ds(1, 3)], 0)
    sent(tok.at[pl.ds(1, 7), 0], 1)
    sent(tok.at[pl.ds(1, 7), 1, 0], 2)
    sent(tok.at[:, 1, pl.ds(1, 3)], 3)
    sent(ins, 4)
    sent(xs, 5)
    sent(slope.at[0, :, :, pl.ds(0, 3)], 6)
    sent(slope.at[0], 7)
    sent(ys, 8)
    sent(ghv.at[0], 10)
    sent(hidv.at[0], 11)
    total = yown[0]
    arrived(zr, m_rs.at[2])
    for j in range(1, NG):
        total = total + zr[j - 1].astype(F32)
    o_gt[...] = total.reshape(32, 1536).astype(BF)
    sent(zs, 9)


def put(hid, gt, gw, gb, o_hid, o_gt, o_gw, o_gb, gb1, sems):
    copies = [pltpu.make_async_copy(src, dst, sems.at[i])
              for i, (src, dst) in enumerate(((gw, o_gw), (hid, o_hid), (gt, o_gt), (gb1, o_gb)))]
    for cp in copies[:3]:
        cp.start()
    for h in range(2):
        gb1[h * W2:(h + 1) * W2] = gb[h, :]
    copies[3].start()
    for cp in copies:
        cp.wait()


def local(tokens, weight, bias, gh):
    any_ = pl.BlockSpec(memory_space=pl.ANY)
    vmem = pl.BlockSpec(memory_space=pltpu.VMEM)
    dma = pltpu.SemaphoreType.DMA
    V = pltpu.VMEM
    held = pl.pallas_call(
        body,
        out_shape=(V((128, 1536), BF), V((32, 1536), BF), V((1536, 1536), BF), V((2, W2), F32)),
        in_specs=[any_] * 4,
        out_specs=(vmem,) * 4,
        scratch_shapes=[
            V((2, 1536, W2), BF), V((2, W2, 1536), BF), V((NG, 2, 4, 16, 1536), BF), V((2, NG, 2, 4, 16, W2), BF),
            V((2, 128, W2), BF), V((2, 128, W2), BF),
            V((NG, 2, 4, 16, W2), F32), V((NG, 2, 4, 16, W2), F32), V((NG, 2, 4, 16, W2), F32), V((NG, 2, 16, W2), F32),
            V((NG, 3, 2, 16, W2), BF), V((NG, 3, 2, 16, W2), BF), V((128, 1536), F32), V((NG, 2, 16, 1536), F32),
            V((NG, 3, 2, 16, 1536), BF), V((NG, 3, 2, 16, 1536), BF),
            V((NG - 1, 2, 16, 1536), BF), V((NG - 1, 2, 16, 1536), BF), V((1, W2), F32), V((2 * W2,), F32),
            dma((12,)), dma((2,)), dma((NG, 3)), dma((NG,)), dma((NG,)),
            dma((9,)), dma((9,)), dma((9,)), dma((9,)), dma((9,)), dma((3,)), dma((6,)),
        ],
        compiler_params=pltpu.CompilerParams(collective_id=0, has_side_effects=True, vmem_limit_bytes=58 * 2**20),
        cost_estimate=pl.CostEstimate(flops=6 * 1024 * 1536 * 1536, bytes_accessed=10 * 2**20, transcendentals=128 * 1536),
        name="layer",
    )(tokens, weight, bias, gh)
    held = [pltpu.with_memory_space_constraint(v, pltpu.VMEM) for v in held]
    return pl.pallas_call(
        put,
        out_shape=(jax.ShapeDtypeStruct((128, 1536), BF), jax.ShapeDtypeStruct((32, 1536), BF),
                   jax.ShapeDtypeStruct((1536, 1536), BF), jax.ShapeDtypeStruct((2 * W2,), F32)),
        in_specs=[vmem] * 4,
        out_specs=(any_,) * 4,
        scratch_shapes=[V((2 * W2,), F32), dma((4,))],
        compiler_params=pltpu.CompilerParams(vmem_limit_bytes=2 * 2**20),
        name="put",
    )(*held)


def solution(mesh):
    in_specs = (P("col", "row"), P("row", "col"), P("col"), P("row", "col"))
    out_specs = (P("row", "col"), P("col", "row"), P("row", "col"), P("col"))
    return jax.shard_map(local, mesh=mesh, in_specs=in_specs, out_specs=out_specs, check_vma=False)
```
